32 devices in a mesh: tile: 8 (over z, x), spec: 4 (over y, core).
Axes of the slice: x: 2, y: 2, z: 4, core: 2. Of those that a mesh axis runs over, the one named last changes fastest.
Arguments:
- adjoint: float32 [128, 8, 32, 128], P('spec', None, 'tile'), may hold values from -6 to 6
- section_first: bfloat16 [8, 8, 128, 128], P('tile'), may hold values from -1 to 2
- section_second: bfloat16 [8, 8, 128, 128], P('tile'), may hold values from -1 to 2
- jacobian: bfloat16 [8, 8, 128, 128], P('tile'), may hold values from -0.5 to 0.5
- pattern: int32 [8, 8, 2, 2], P('tile'), may hold values 0 or 1
- counts: int32 [8, 8], P('tile'), may hold values from 1 to 512, as said below
- courant: float32 [8, 32, 128], P(None, 'tile'), may hold values from -0.45 to 0.45
- seam_codes: int32 [8, 2], P('tile'), may hold values from 0 to 1, as said below
Outputs:
- adjoint_out: float32 [128, 8, 32, 128], P('spec', None, 'tile')
The draws below stay inside these ranges and needn't reach their ends.
Inputs may be any that keep to these rules, and one draw needn't show every extreme that they name: The active cells of tile t and level l are the first counts[t, l] of its 4 x 128 cells in row-major order. `seam_codes`: column 0 of tile t is the code of the seam between tile t and tile t + 1, column 1 that of the seam between tile t - 1 and tile t (cyclically); a 1 means that the seam reverses the order of cells along it. `pattern`: 1 where a block is present.
All inputs are finite; a program needn't handle non-finite values.
Results may differ from the reference program's by a relative error of at most 0.004.
Values may be sent and summed in bfloat16 or wider, within the bound.
A program may use at most 64 MiB of HBM per device.

```python
import math
import jax
import jax.numpy as jnp

SPECIES = 128
BLK = 64
LEV = 8
CX = 4
CY = 128
NSUB = 4
TILES = 8
NX = 32
NBLK = 2


def make_factor(key, salt, uniform_law):
    sub_key = jax.random.fold_in(key, salt)
    full_shape = (TILES, LEV, SPECIES, SPECIES)
    if uniform_law:
        noise_draw = jax.random.uniform(sub_key, full_shape, jnp.float32, -1.7320508, 1.7320508)
    else:
        noise_draw = jax.random.normal(sub_key, full_shape, jnp.float32)
    identity = jnp.eye(SPECIES, dtype=jnp.float32)
    return (identity[None, None] + 0.5 * noise_draw / math.sqrt(SPECIES)).astype(jnp.bfloat16)


def draw_section_first(key, part):
    return make_factor(key, 11, False)


def draw_section_second(key, part):
    return make_factor(key, 13, False)


def draw_counts(key, part):
    total_slots = TILES * LEV
    count_draw = jax.random.randint(jax.random.fold_in(key, 31), (total_slots,), 1, CX * CY + 1)
    first_slot = jax.random.randint(jax.random.fold_in(key, 37), (), 0, total_slots)
    offset_slot = jax.random.randint(jax.random.fold_in(key, 41), (), 0, total_slots - 1)
    second_slot = (first_slot + 1 + offset_slot) % total_slots
    count_draw = count_draw.at[second_slot].set(1)
    count_draw = count_draw.at[first_slot].set(CX * CY)
    return count_draw.reshape(TILES, LEV).astype(jnp.int32)


def draw_seam_codes(key, part):
    seam_flags = jax.random.randint(jax.random.fold_in(key, 23), (TILES,), 0, 2)
    return jnp.stack([seam_flags, jnp.roll(seam_flags, 1)], axis=1).astype(jnp.int32)


def touch_ends(array, stream_key, low, largest):
    longest = array.shape.index(max(array.shape))
    spots = []
    for shift in (0, 1):
        where = [jax.random.randint(jax.random.fold_in(stream_key, axis), (), 0, length) for axis, length in enumerate(array.shape)]
        where[longest] = (where[longest] + shift) % array.shape[longest]
        spots.append(tuple(where))
    return array.at[spots[0]].set(low).at[spots[1]].set(largest)


def level_of(stream_key, extent, shards, smallest, largest):
    level = 1.0
    for position, blocks in shards:
        heights = jax.random.uniform(jax.random.fold_in(jax.random.fold_in(stream_key, 6), position), (blocks,), jnp.float32, smallest / len(shards), largest / len(shards))
        level = level * jnp.repeat(jnp.exp(heights), extent[position] // blocks).reshape((-1,) + (1,) * (len(extent) - 1 - position))
    return level


def bell_draw(rng, dims, spread, most, shards=(), kind=jnp.bfloat16):
    result = jax.random.normal(rng, dims, jnp.float32) * spread
    if len(shards) > 0:
        result = level_of(rng, dims, shards, -0.22, 0.18) * result
    return jnp.clip(result, min=-most, max=most).astype(kind)


def setup_inputs(seed: int = 0) -> dict:
    key_of = jax.random.split(jax.random.key(seed), 9)
    adjoint = bell_draw(key_of[0], (SPECIES, LEV, NX, CY), 1.0, 6.0, ((0, 4), (2, 8)), jnp.float32)
    section_first = draw_section_first(jax.random.fold_in(key_of[8], 71), 0)
    section_second = draw_section_second(jax.random.fold_in(key_of[8], 71), 0)
    jacobian = bell_draw(key_of[3], (TILES, LEV, SPECIES, SPECIES), SPECIES ** -0.5, 0.5, ((0, 8),))
    pattern = touch_ends((jax.random.randint(key_of[4], (TILES, LEV, NBLK, NBLK), 0, 4) < 3).astype(jnp.int32), jax.random.fold_in(key_of[4], 1), 0, 1)
    counts = draw_counts(jax.random.fold_in(key_of[8], 71), 0)
    courant = jnp.clip(jax.random.uniform(key_of[6], (LEV, NX, CY), jnp.float32, -0.45, 0.45) * level_of(key_of[6], (LEV, NX, CY), ((1, 8),), -0.4, 0.0), -0.45, 0.45)
    seam_codes = draw_seam_codes(jax.random.fold_in(key_of[8], 71), 0)
    return {"adjoint": adjoint, "section_first": section_first, "section_second": section_second, "jacobian": jacobian, "pattern": pattern, "counts": counts, "courant": courant, "seam_codes": seam_codes}


section_weights = (0.4, 0.3, 0.2, 0.1)
coupling = 0.5


def transposed(matrix, field_tiles):
    return jnp.einsum("tlsp,sltc->pltc", matrix.astype(jnp.float32), field_tiles.astype(jnp.float32))


def reference(adjoint, section_first, section_second, jacobian, pattern, counts, courant, seam_codes):
    cell_count = CX * CY
    field_tiles = adjoint.reshape(SPECIES, LEV, TILES, cell_count)
    rounded = field_tiles.astype(jnp.bfloat16)
    present = jnp.repeat(jnp.repeat(pattern, BLK, axis=2), BLK, axis=3) == 1
    jac_used = jnp.where(present, jacobian, jnp.zeros_like(jacobian))
    start_wide = rounded.astype(jnp.float32)
    first_y = transposed(section_first, rounded).astype(jnp.bfloat16)
    section_u = transposed(section_second, first_y).astype(jnp.bfloat16)
    running_sum = None
    for section in range(4):
        coupled = transposed(jac_used, section_u)
        if section == 0:
            running_sum = section_weights[0] * coupled
        else:
            running_sum = running_sum + section_weights[section] * coupled
        if section < 3:
            mixed_term = (start_wide + coupling * coupled).astype(jnp.bfloat16)
            first_y = transposed(section_first, mixed_term).astype(jnp.bfloat16)
            section_u = transposed(section_second, first_y).astype(jnp.bfloat16)
    chemistry = running_sum.astype(jnp.bfloat16).astype(jnp.float32)
    cell_index = jnp.arange(cell_count, dtype=jnp.int32)
    active_mask = cell_index[None, None, :] < jnp.transpose(counts)[:, :, None]
    adjoint_state = field_tiles + jnp.where(active_mask[None], chemistry, jnp.zeros_like(chemistry))
    adjoint_state = adjoint_state.reshape(SPECIES, LEV, NX, CY)
    row_index = jnp.arange(NX, dtype=jnp.int32)
    owner_tile = row_index // CX
    flip_up = (row_index % CX == CX - 1) & (seam_codes[owner_tile, 0] == 1)
    flip_down = (row_index % CX == 0) & (seam_codes[owner_tile, 1] == 1)
    lower_faces = jnp.roll(courant, 1, axis=1)
    lower_faces = jnp.where(flip_down[None, :, None], lower_faces[..., ::-1], lower_faces)
    rising = jnp.maximum(courant, 0.0)
    falling = jnp.minimum(lower_faces, 0.0)
    for substep in range(NSUB):
        above_cells = jnp.roll(adjoint_state, -1, axis=2)
        above_cells = jnp.where(flip_up[None, None, :, None], above_cells[..., ::-1], above_cells)
        below_cells = jnp.roll(adjoint_state, 1, axis=2)
        below_cells = jnp.where(flip_down[None, None, :, None], below_cells[..., ::-1], below_cells)
        adjoint_state = adjoint_state + rising * (above_cells - adjoint_state) + falling * (adjoint_state - below_cells)
    return adjoint_state
```

```python
import functools

import jax
import jax.numpy as jnp
from jax import lax
from jax.experimental import pallas as pl
from jax.experimental.pallas import tpu as pltpu
from jax.sharding import PartitionSpec as P

NSUB = 4

section_weights = (0.4, 0.3, 0.2, 0.1)
coupling = 0.5

MESH = pl.DeviceIdType.MESH
F32 = jnp.float32
BF16 = jnp.bfloat16


def power_weights():
    out = []
    for j in range(4):
        out.append((coupling**j) * sum(section_weights[j:]))
    return out


def dot(a, b):
    return jnp.dot(a, b, preferred_element_type=F32)


def split(x):
    hi = x.astype(BF16)
    return hi, (x - hi.astype(F32)).astype(BF16)


def kernel(
    tiles, specs, levels, rows, species_dev, blocks,
    adj_hbm, first_hbm, second_hbm, jac_hbm, cour, pattern, counts, codes,
    out,
    adj, mats, abuf, gath, ebuf, emat, sbuf, side, state, ret, rbuf,
    load_sem, a_send, a_recv, e_send, e_recv, s_send, s_recv, r_send, r_recv,
):
    seam = adj.shape[1]
    species = specs * species_dev
    cells = rows * seam
    stride = levels * rows
    pairs = tiles // 2
    t = lax.axis_index("tile")
    s = lax.axis_index("spec")
    z = t // 2
    p = t - 2 * z
    zn = lax.rem(z + pairs - 1 + 2 * p, pairs)
    slot_own = 1 + p
    slot_other = 2 - p
    slot_far = 3 * (1 - p)
    own_level = 2 * s + p

    adj_copy = pltpu.make_async_copy(adj_hbm, adj, load_sem.at[0])
    adj_copy.start()
    mat_copies = []
    for i, ref in enumerate((first_hbm, second_hbm, jac_hbm)):
        copy = pltpu.make_async_copy(ref.at[0, pl.ds(2 * s, 2)], mats.at[i], load_sem.at[1 + i])
        copy.start()
        mat_copies.append(copy)

    barrier = pltpu.get_barrier_semaphore()
    for d in range(1, levels):
        lev = lax.rem(own_level + d, levels)
        pl.semaphore_signal(barrier, inc=1, device_id=(2 * z + lax.rem(lev, 2), lev // 2), device_id_type=MESH)
    for src in range(specs):
        below = lax.rem(2 * z + tiles - 1, tiles)
        above = lax.rem(2 * z + 2, tiles)
        for q in (below, above):
            pl.semaphore_signal(barrier, inc=1, device_id=(q, src), device_id_type=MESH)

    side_rows = sbuf.shape[1]
    row_id = lax.broadcasted_iota(jnp.int32, (side_rows, seam), 0)
    for q in range(2):
        packed = jnp.where(row_id == rows, codes[0, 0].astype(F32), 0.0)
        packed = jnp.where(row_id == rows + 1, codes[0, 1].astype(F32), packed)
        packed = jnp.where(row_id == rows + 2, counts[0, 2 * s + q].astype(F32), packed)
        sbuf[q] = packed
        sbuf[q, 0:rows, :] = cour[2 * s + q]
    adj_copy.wait()
    for lev in range(levels):
        for r in range(rows):
            abuf[lev, r] = adj[pl.ds(lev * rows + r, species_dev, stride), :].astype(BF16)

    pl.semaphore_wait(barrier, 2 * levels - 1)

    sends = []

    def send(src, dst, send_sem, recv_sem, device):
        copy = pltpu.make_async_remote_copy(
            src_ref=src, dst_ref=dst, send_sem=send_sem, recv_sem=recv_sem,
            device_id=device, device_id_type=MESH,
        )
        copy.start()
        sends.append(copy)

    def owner(pair, lev):
        return (2 * pair + lax.rem(lev, 2), lev // 2)

    for d in range(levels):
        lev = lax.rem(own_level + d, levels)
        send(abuf.at[lev], gath.at[slot_far, s], a_send.at[0, d], a_recv.at[slot_far, s], owner(zn, lev))
        if d > 0:
            send(abuf.at[lev], gath.at[slot_own, s], a_send.at[1, d], a_recv.at[slot_own, s], owner(z, lev))
    targets = ((1 - p, (2 * z + 1 - p, s), slot_own), (0, (2 * zn, s), slot_far), (1, (2 * zn + 1, s), slot_far))
    for i, (q, device, slot) in enumerate(targets):
        send(sbuf.at[q], side.at[slot], s_send.at[i], s_recv.at[slot], device)

    gath[slot_own, s] = abuf[own_level]
    side[slot_own] = sbuf[p]

    for copy in mat_copies:
        copy.wait()
    weights = power_weights()
    block = species // blocks
    row_s = lax.broadcasted_iota(jnp.int32, (species, species), 0)
    col_s = lax.broadcasted_iota(jnp.int32, (species, species), 1)
    jac_used = []
    for q in range(2):
        present = jnp.zeros((species, species), jnp.int32)
        for b in range(blocks):
            for e in range(blocks):
                inside = (
                    (row_s >= b * block) & (row_s < (b + 1) * block)
                    & (col_s >= e * block) & (col_s < (e + 1) * block)
                )
                present = jnp.where(inside, pattern[0, 2 * s + q, b, e], present)
        jac_used.append(jnp.where(present == 1, mats[2, q].astype(F32), 0.0).astype(BF16))
    both = [split(dot(mats[0, q], mats[1, q])) for q in range(2)]
    g = [dot(both[q][0], jac_used[q]) + dot(both[q][1], jac_used[q]) for q in range(2)]
    gh = [g[q].astype(BF16) for q in range(2)]
    acc = [weights[2] * g[q] + weights[3] * dot(gh[q], gh[q]) for q in range(2)]
    acc = [weights[1] * g[q] + dot(gh[q], acc[q].astype(BF16)) for q in range(2)]
    acc = [weights[0] * g[q] + dot(gh[q], acc[q].astype(BF16)) for q in range(2)]
    for q in range(2):
        ebuf[q] = jnp.transpose(acc[q]).astype(BF16)
    for i, (q, device, slot) in enumerate(targets):
        send(ebuf.at[q], emat.at[slot], e_send.at[i], e_recv.at[slot], device)
    emat[slot_own] = ebuf[p]

    def arrived(dst, sem):
        pltpu.make_async_copy(dst, dst, sem).wait()

    for slot in (slot_other, 0, 3):
        arrived(side.at[slot], s_recv.at[slot])

    code_up1 = side[1, rows : rows + 1, :]
    code_down1 = side[1, rows + 1 : rows + 2, :]
    code_up2 = side[2, rows : rows + 1, :]
    flips = [code_down1, jnp.zeros_like(code_up1), code_up1, jnp.abs(code_up1 - code_up2)]
    row_y = lax.broadcasted_iota(jnp.int32, (seam, seam), 0)
    col_y = lax.broadcasted_iota(jnp.int32, (seam, seam), 1)
    eye = jnp.where(row_y == col_y, 1.0, 0.0)
    anti = jnp.where(row_y + col_y == seam - 1, 1.0, 0.0)
    perms = [(eye + (anti - eye) * flips[k]).astype(BF16) for k in range(4)]
    faces = []
    for k in range(4):
        block_k = side[k]
        if k != 1:
            hi = block_k.astype(BF16)
            rest = block_k - hi.astype(F32)
            mid = rest.astype(BF16)
            low = (rest - mid.astype(F32)).astype(BF16)
            block_k = dot(hi, perms[k]) + dot(mid, perms[k]) + dot(low, perms[k])
        for r in range(rows):
            faces.append(block_k[r : r + 1, :])

    lane = lax.broadcasted_iota(jnp.int32, (1, seam), 1).astype(F32)

    for slot in (slot_other, 0, 3):
        arrived(emat.at[slot], e_recv.at[slot])
    for d in range(1, specs):
        src = lax.rem(s + d, specs)
        arrived(gath.at[slot_own, src], a_recv.at[slot_own, src])
    for src in range(specs):
        for slot in (slot_other, 0, 3):
            arrived(gath.at[slot, src], a_recv.at[slot, src])

    for k in (1, 2, 0, 3):
        field = [[gath[k, src, r] for src in range(specs)] for r in range(rows)]
        field = [jnp.concatenate(parts, axis=0) for parts in field]
        if k != 1:
            turned = dot(jnp.concatenate(field, axis=0), perms[k]).astype(BF16)
            field = [turned[r * species : (r + 1) * species] for r in range(rows)]
        chem = dot(emat[k], jnp.concatenate(field, axis=1))
        count = side[k, rows + 2 : rows + 3, :]
        place = lane + flips[k] * (seam - 1 - 2 * lane)
        for r in range(rows):
            active = (place + float(r * seam)) < count
            term = chem[:, r * seam : (r + 1) * seam]
            state[k * rows + r] = field[r].astype(F32) + jnp.where(active, term, 0.0)

    total = 4 * rows
    group = 16
    shape = (group, seam)
    per_dev = species_dev // group

    def advect(i, carry):
        at = pl.multiple_of(i * group, group)
        a = [state[r, pl.ds(at, group), :] for r in range(total)]
        for step in range(1, NSUB + 1):
            new = list(a)
            for r in range(step, total - step):
                rising = jnp.maximum(faces[r], 0.0)
                falling = jnp.minimum(faces[r - 1], 0.0)
                new[r] = a[r] + rising * (a[r + 1] - a[r]) + falling * (a[r] - a[r - 1])
            a = new
        who = i // per_dev
        within = pl.multiple_of((i - who * per_dev) * group, group)
        for r in range(rows):
            ret[0, who, r, pl.ds(within, group), :] = a[rows + r].astype(BF16)
        upper = jnp.concatenate([a[2 * rows + r] for r in range(rows)], axis=0).astype(BF16)
        upper = dot(upper, perms[2]).astype(BF16)
        for r in range(rows):
            ret[1, who, r, pl.ds(within, group), :] = upper[r * group : (r + 1) * group]
        return carry

    lax.fori_loop(0, species // group, advect, 0)

    for d in range(1, levels):
        lev = lax.rem(own_level + d, levels)
        q = lax.rem(lev, 2)
        send(ret.at[q, lev // 2], rbuf.at[own_level], r_send.at[d], r_recv.at[own_level], owner(z, lev))
    rbuf[own_level] = ret[p, s]
    for d in range(1, levels):
        lev = lax.rem(own_level + d, levels)
        arrived(rbuf.at[lev], r_recv.at[lev])
    for lev in range(levels):
        for r in range(rows):
            out[pl.ds(lev * rows + r, species_dev, stride), :] = rbuf[lev, r].astype(F32)
    for copy in sends:
        copy.wait_send()


def shards(tiles, specs, adjoint, section_first, section_second, jacobian, pattern, counts, courant, seam_codes):
    species_dev, levels, rows, seam = adjoint.shape
    species = jacobian.shape[2]
    assert levels == 2 * specs and tiles % 2 == 0 and rows >= NSUB
    side_rows = (rows + 3 + 7) // 8 * 8
    dma = pltpu.SemaphoreType.DMA
    out = pl.pallas_call(
        functools.partial(kernel, tiles, specs, levels, rows, species_dev, pattern.shape[2]),
        out_shape=jax.ShapeDtypeStruct((species_dev * levels * rows, seam), F32),
        in_specs=[pl.BlockSpec(memory_space=pl.ANY)] * 4
        + [pl.BlockSpec(memory_space=pltpu.VMEM)]
        + [pl.BlockSpec(memory_space=pltpu.SMEM)] * 3,
        out_specs=pl.BlockSpec(memory_space=pltpu.VMEM),
        scratch_shapes=[
            pltpu.VMEM((species_dev * levels * rows, seam), F32),
            pltpu.VMEM((3, 2, species, species), BF16),
            pltpu.VMEM((levels, rows, species_dev, seam), BF16),
            pltpu.VMEM((4, specs, rows, species_dev, seam), BF16),
            pltpu.VMEM((2, species, species), BF16),
            pltpu.VMEM((4, species, species), BF16),
            pltpu.VMEM((2, side_rows, seam), F32),
            pltpu.VMEM((4, side_rows, seam), F32),
            pltpu.VMEM((4 * rows, species, seam), F32),
            pltpu.VMEM((2, specs, rows, species_dev, seam), BF16),
            pltpu.VMEM((levels, rows, species_dev, seam), BF16),
            dma((4,)),
            dma((2, levels)),
            dma((4, specs)),
            dma((3,)),
            dma((4,)),
            dma((3,)),
            dma((4,)),
            dma((levels,)),
            dma((levels,)),
        ],
        compiler_params=pltpu.CompilerParams(
            collective_id=0, has_side_effects=True, vmem_limit_bytes=32 * 1024 * 1024
        ),
    )(
        adjoint.reshape(species_dev * levels * rows, seam),
        section_first, section_second, jacobian, courant, pattern, counts, seam_codes,
    )
    return out.reshape(species_dev, levels, rows, seam)


def solution(mesh):
    in_specs = (
        P("spec", None, "tile", None),
        P("tile", None, None, None),
        P("tile", None, None, None),
        P("tile", None, None, None),
        P("tile", None, None, None),
        P("tile", None),
        P(None, "tile", None),
        P("tile", None),
    )
    out_specs = P("spec", None, "tile", None)
    body = functools.partial(shards, mesh.shape["tile"], mesh.shape["spec"])
    return jax.shard_map(body, mesh=mesh, in_specs=in_specs, out_specs=out_specs, check_vma=False)
```

```python
import functools

import jax
import jax.numpy as jnp
from jax import lax
from jax.experimental import pallas as pl
from jax.experimental.pallas import tpu as pltpu
from jax.sharding import PartitionSpec as P

NSUB = 4

section_weights = (0.4, 0.3, 0.2, 0.1)
coupling = 0.5

MESH = pl.DeviceIdType.MESH
F32 = jnp.float32
BF16 = jnp.bfloat16


def power_weights():
    out = []
    for j in range(4):
        out.append((coupling**j) * sum(section_weights[j:]))
    return out


def dot(a, b):
    return jnp.dot(a, b, preferred_element_type=F32)


def split(x):
    hi = x.astype(BF16)
    return hi, (x - hi.astype(F32)).astype(BF16)


def twice(x):
    return jnp.concatenate([x, x], axis=0)


def kernel(
    tiles, specs, levels, rows, species_dev, blocks,
    adj_hbm, first_hbm, second_hbm, jac_hbm, cour_hbm, pattern_hbm, counts_hbm, codes_hbm,
    out,
    adj, mats, cour, pattern, counts, codes, abuf, gath, ebuf, emat, sbuf, side, state, ret,
    load_sem, own_sem, a_send, a_recv, e_send, e_recv, s_send, s_recv, r_send, r_recv,
):
    seam = adj.shape[1]
    species = specs * species_dev
    cells = rows * seam
    stride = levels * rows
    pairs = tiles // 2
    t = lax.axis_index("tile")
    s = lax.axis_index("spec")
    z = t // 2
    p = t - 2 * z
    zn = lax.rem(z + pairs - 1 + 2 * p, pairs)
    slot_own = 1 + p
    slot_other = 2 - p
    slot_far = 3 * (1 - p)
    own_level = 2 * s + p

    adj_copy = pltpu.make_async_copy(adj_hbm, adj, load_sem.at[0])
    adj_copy.start()
    small_copies = []
    for i, (ref, to) in enumerate(
        ((cour_hbm, cour), (counts_hbm, counts), (codes_hbm, codes), (pattern_hbm, pattern))
    ):
        copy = pltpu.make_async_copy(ref, to, load_sem.at[4 + i])
        copy.start()
        small_copies.append(copy)
    mat_copies = []
    for i, ref in enumerate((first_hbm, second_hbm, jac_hbm)):
        copy = pltpu.make_async_copy(ref.at[0, pl.ds(2 * s, 2)], mats.at[i], load_sem.at[1 + i])
        copy.start()
        mat_copies.append(copy)

    barrier = pltpu.get_barrier_semaphore()
    for d in range(1, levels):
        lev = lax.rem(own_level + d, levels)
        pl.semaphore_signal(barrier, inc=1, device_id=(2 * z + lax.rem(lev, 2), lev // 2), device_id_type=MESH)
    for src in range(specs):
        below = lax.rem(2 * z + tiles - 1, tiles)
        above = lax.rem(2 * z + 2, tiles)
        for q in (below, above):
            pl.semaphore_signal(barrier, inc=1, device_id=(q, src), device_id_type=MESH)

    for copy in small_copies:
        copy.wait()
    side_rows = sbuf.shape[1]
    row_id = lax.broadcasted_iota(jnp.int32, (side_rows, seam), 0)
    for q in range(2):
        packed = jnp.where(row_id == rows, codes[0, 0].astype(F32), 0.0)
        packed = jnp.where(row_id == rows + 1, codes[0, 1].astype(F32), packed)
        packed = jnp.where(row_id == rows + 2, counts[0, 2 * s + q].astype(F32), packed)
        sbuf[q] = packed
        sbuf[q, 0:rows, :] = cour[2 * s + q]
    adj_copy.wait()
    for lev in range(levels):
        for r in range(rows):
            abuf[lev, r] = adj[pl.ds(lev * rows + r, species_dev, stride), :].astype(BF16)

    pl.semaphore_wait(barrier, 2 * levels - 1)

    sends = []

    def send(src, dst, send_sem, recv_sem, device):
        copy = pltpu.make_async_remote_copy(
            src_ref=src, dst_ref=dst, send_sem=send_sem, recv_sem=recv_sem,
            device_id=device, device_id_type=MESH,
        )
        copy.start()
        sends.append(copy)

    def owner(pair, lev):
        return (2 * pair + lax.rem(lev, 2), lev // 2)

    targets = ((1 - p, (2 * z + 1 - p, s), slot_own), (0, (2 * zn, s), slot_far), (1, (2 * zn + 1, s), slot_far))
    for i, (q, device, slot) in enumerate(targets):
        send(sbuf.at[q], side.at[slot], s_send.at[i], s_recv.at[slot], device)
    for d in range(levels):
        lev = lax.rem(own_level + d, levels)
        send(abuf.at[lev], gath.at[slot_far, s], a_send.at[0, d], a_recv.at[slot_far, s], owner(zn, lev))

    gath[slot_own, s] = abuf[own_level]
    side[slot_own] = sbuf[p]

    for copy in mat_copies:
        copy.wait()
    weights = power_weights()
    block = species // blocks
    row_s = lax.broadcasted_iota(jnp.int32, (species, species), 0)
    col_s = lax.broadcasted_iota(jnp.int32, (species, species), 1)
    jac_used = []
    for q in range(2):
        present = jnp.zeros((species, species), jnp.int32)
        for b in range(blocks):
            for e in range(blocks):
                inside = (
                    (row_s >= b * block) & (row_s < (b + 1) * block)
                    & (col_s >= e * block) & (col_s < (e + 1) * block)
                )
                present = jnp.where(inside, pattern[0, b, e, 2 * s + q], present)
        jac_used.append(jnp.where(present == 1, mats[2, q].astype(F32), 0.0).astype(BF16))
    both = [jnp.concatenate(split(dot(mats[0, q], mats[1, q])), axis=1) for q in range(2)]
    g = [dot(both[q], twice(jac_used[q])) for q in range(2)]
    both = [jnp.concatenate(split(g[q]), axis=1) for q in range(2)]
    acc = [weights[2] * g[q] + weights[3] * dot(both[q], twice(g[q].astype(BF16))) for q in range(2)]
    acc = [weights[1] * g[q] + dot(both[q], twice(acc[q].astype(BF16))) for q in range(2)]
    acc = [weights[0] * g[q] + dot(both[q], twice(acc[q].astype(BF16))) for q in range(2)]
    for q in range(2):
        ebuf[q] = jnp.transpose(acc[q]).astype(BF16)
    for i, (q, device, slot) in enumerate(targets):
        send(ebuf.at[q], emat.at[slot], e_send.at[i], e_recv.at[slot], device)
    for d in range(1, levels):
        lev = lax.rem(own_level + d, levels)
        send(abuf.at[lev], gath.at[slot_own, s], a_send.at[1, d], a_recv.at[slot_own, s], owner(z, lev))
    emat[slot_own] = ebuf[p]

    def arrived(dst, sem):
        pltpu.make_async_copy(dst, dst, sem).wait()

    for slot in (slot_other, 0, 3):
        arrived(side.at[slot], s_recv.at[slot])

    code_up1 = side[1, rows : rows + 1, :]
    code_down1 = side[1, rows + 1 : rows + 2, :]
    code_up2 = side[2, rows : rows + 1, :]
    flips = [code_down1, jnp.zeros_like(code_up1), code_up1, jnp.abs(code_up1 - code_up2)]
    row_y = lax.broadcasted_iota(jnp.int32, (seam, seam), 0)
    col_y = lax.broadcasted_iota(jnp.int32, (seam, seam), 1)
    eye = jnp.where(row_y == col_y, 1.0, 0.0)
    anti = jnp.where(row_y + col_y == seam - 1, 1.0, 0.0)
    perms = [(eye + (anti - eye) * flips[k]).astype(BF16) for k in range(4)]
    faces = []
    for k in range(4):
        block_k = side[k]
        if k != 1:
            hi = block_k.astype(BF16)
            rest = block_k - hi.astype(F32)
            mid = rest.astype(BF16)
            low = (rest - mid.astype(F32)).astype(BF16)
            block_k = dot(hi, perms[k]) + dot(mid, perms[k]) + dot(low, perms[k])
        for r in range(rows):
            faces.append(block_k[r : r + 1, :])

    lane = lax.broadcasted_iota(jnp.int32, (1, seam), 1).astype(F32)

    for k in (1, 2, 0, 3):
        if k == 1:
            arrived(emat.at[slot_other], e_recv.at[slot_other])
            for d in range(1, specs):
                src = lax.rem(s + d, specs)
                arrived(gath.at[slot_own, src], a_recv.at[slot_own, src])
            for src in range(specs):
                arrived(gath.at[slot_other, src], a_recv.at[slot_other, src])
        elif k != 2:
            arrived(emat.at[k], e_recv.at[k])
            for src in range(specs):
                arrived(gath.at[k, src], a_recv.at[k, src])
        field = [[gath[k, src, r] for src in range(specs)] for r in range(rows)]
        field = [jnp.concatenate(parts, axis=0) for parts in field]
        if k != 1:
            turned = dot(jnp.concatenate(field, axis=0), perms[k]).astype(BF16)
            field = [turned[r * species : (r + 1) * species] for r in range(rows)]
        chem = dot(emat[k], jnp.concatenate(field, axis=1))
        count = side[k, rows + 2 : rows + 3, :]
        place = lane + flips[k] * (seam - 1 - 2 * lane)
        for r in range(rows):
            active = (place + float(r * seam)) < count
            term = chem[:, r * seam : (r + 1) * seam]
            state[k * rows + r] = field[r].astype(F32) + jnp.where(active, term, 0.0)

    total = 4 * rows
    group = 16
    shape = (group, seam)

    def advect(who, within):
        at = pl.multiple_of(who * species_dev + within, group)
        a = [state[r, pl.ds(at, group), :] for r in range(total)]
        for step in range(1, NSUB + 1):
            new = list(a)
            for r in range(step, total - step):
                rising = jnp.maximum(faces[r], 0.0)
                falling = jnp.minimum(faces[r - 1], 0.0)
                new[r] = a[r] + rising * (a[r + 1] - a[r]) + falling * (a[r] - a[r - 1])
            a = new
        for r in range(rows):
            ret[0, who, r, within : within + group, :] = a[rows + r].astype(BF16)
        upper = jnp.concatenate([a[2 * rows + r] for r in range(rows)], axis=0).astype(BF16)
        upper = dot(upper, perms[2]).astype(BF16)
        for r in range(rows):
            ret[1, who, r, within : within + group, :] = upper[r * group : (r + 1) * group]

    for i in range(specs):
        who = lax.rem(s + 1 + i, specs)
        for within in range(0, species_dev, group):
            advect(who, within)
        for j in range(2):
            q = lax.rem(p + 1 + j, 2)
            if i < specs - 1 or j == 0:
                send(ret.at[q, who], out.at[own_level], r_send.at[2 * i + j], r_recv.at[own_level], (2 * z + q, who))
    own_copy = pltpu.make_async_copy(ret.at[p, s], out.at[own_level], own_sem)
    own_copy.start()
    for d in range(1, levels):
        lev = lax.rem(own_level + d, levels)
        arrived(out.at[lev], r_recv.at[lev])
    own_copy.wait()
    for copy in sends:
        copy.wait_send()


def shards(tiles, specs, adjoint, section_first, section_second, jacobian, pattern, counts, courant, seam_codes):
    species_dev, levels, rows, seam = adjoint.shape
    species = jacobian.shape[2]
    assert levels == 2 * specs and tiles % 2 == 0 and rows >= NSUB
    side_rows = (rows + 3 + 7) // 8 * 8
    dma = pltpu.SemaphoreType.DMA
    out = pl.pallas_call(
        functools.partial(kernel, tiles, specs, levels, rows, species_dev, pattern.shape[2]),
        out_shape=jax.ShapeDtypeStruct((levels, rows, species_dev, seam), BF16),
        in_specs=[pl.BlockSpec(memory_space=pl.ANY)] * 8,
        out_specs=pl.BlockSpec(memory_space=pl.ANY),
        scratch_shapes=[
            pltpu.VMEM((species_dev * levels * rows, seam), F32),
            pltpu.VMEM((3, 2, species, species), BF16),
            pltpu.VMEM(courant.shape, F32),
            pltpu.SMEM((1,) + pattern.shape[2:] + (levels,), jnp.int32),
            pltpu.SMEM(counts.shape, jnp.int32),
            pltpu.SMEM(seam_codes.shape, jnp.int32),
            pltpu.VMEM((levels, rows, species_dev, seam), BF16),
            pltpu.VMEM((4, specs, rows, species_dev, seam), BF16),
            pltpu.VMEM((2, species, species), BF16),
            pltpu.VMEM((4, species, species), BF16),
            pltpu.VMEM((2, side_rows, seam), F32),
            pltpu.VMEM((4, side_rows, seam), F32),
            pltpu.VMEM((4 * rows, species, seam), F32),
            pltpu.VMEM((2, specs, rows, species_dev, seam), BF16),
            dma((8,)),
            dma(()),
            dma((2, levels)),
            dma((4, specs)),
            dma((3,)),
            dma((4,)),
            dma((3,)),
            dma((4,)),
            dma((levels,)),
            dma((levels,)),
        ],
        compiler_params=pltpu.CompilerParams(
            collective_id=0, has_side_effects=True, vmem_limit_bytes=60 * 1024 * 1024
        ),
    )(
        adjoint.reshape(species_dev * levels * rows, seam),
        section_first, section_second, jacobian, courant, jnp.transpose(pattern, (0, 2, 3, 1)), counts, seam_codes,
    )
    return jnp.transpose(out, (2, 0, 1, 3)).astype(F32)


def solution(mesh):
    in_specs = (
        P("spec", None, "tile", None),
        P("tile", None, None, None),
        P("tile", None, None, None),
        P("tile", None, None, None),
        P("tile", None, None, None),
        P("tile", None),
        P(None, "tile", None),
        P("tile", None),
    )
    out_specs = P("spec", None, "tile", None)
    body = functools.partial(shards, mesh.shape["tile"], mesh.shape["spec"])
    return jax.shard_map(body, mesh=mesh, in_specs=in_specs, out_specs=out_specs, check_vma=False)
```

```python
import functools

import jax
import jax.numpy as jnp
from jax import lax
from jax.experimental import pallas as pl
from jax.experimental.pallas import tpu as pltpu
from jax.sharding import PartitionSpec as P

NSUB = 4

section_weights = (0.4, 0.3, 0.2, 0.1)
coupling = 0.5

MESH = pl.DeviceIdType.MESH
F32 = jnp.float32
BF16 = jnp.bfloat16


def power_weights():
    out = []
    for j in range(4):
        out.append((coupling**j) * sum(section_weights[j:]))
    return out


def dot(a, b):
    return jnp.dot(a, b, preferred_element_type=F32)


def split(x):
    hi = x.astype(BF16)
    return hi, (x - hi.astype(F32)).astype(BF16)


def twice(x):
    return jnp.concatenate([x, x], axis=0)


def kernel(
    tiles, specs, levels, rows, species_dev, blocks,
    adj_hbm, first_hbm, second_hbm, jac_hbm, cour_hbm, pattern_hbm, counts_hbm, codes_hbm,
    out,
    adj, mats, cour, pattern, counts, codes, abuf, gath, ebuf, emat, sbuf, side, state, ret,
    load_sem, own_sem, a_send, a_recv, e_send, e_recv, s_send, s_recv, r_send, r_recv,
):
    seam = adj.shape[1]
    species = specs * species_dev
    cells = rows * seam
    stride = levels * rows
    pairs = tiles // 2
    t = lax.axis_index("tile")
    s = lax.axis_index("spec")
    z = t // 2
    p = t - 2 * z
    zn = lax.rem(z + pairs - 1 + 2 * p, pairs)
    slot_own = 1 + p
    slot_other = 2 - p
    slot_far = 3 * (1 - p)
    own_level = 2 * s + p

    adj_copy = pltpu.make_async_copy(adj_hbm, adj, load_sem.at[0])
    adj_copy.start()
    small_copies = []
    for i, (ref, to) in enumerate(
        ((cour_hbm, cour), (counts_hbm, counts), (codes_hbm, codes), (pattern_hbm, pattern))
    ):
        copy = pltpu.make_async_copy(ref, to, load_sem.at[4 + i])
        copy.start()
        small_copies.append(copy)
    mat_copies = []
    for i, ref in enumerate((first_hbm, second_hbm, jac_hbm)):
        copy = pltpu.make_async_copy(ref.at[0, pl.ds(2 * s, 2)], mats.at[i], load_sem.at[1 + i])
        copy.start()
        mat_copies.append(copy)

    barrier = pltpu.get_barrier_semaphore()
    for d in range(1, levels):
        lev = lax.rem(own_level + d, levels)
        pl.semaphore_signal(barrier, inc=1, device_id=(2 * z + lax.rem(lev, 2), lev // 2), device_id_type=MESH)
    for src in range(specs):
        below = lax.rem(2 * z + tiles - 1, tiles)
        above = lax.rem(2 * z + 2, tiles)
        for q in (below, above):
            pl.semaphore_signal(barrier, inc=1, device_id=(q, src), device_id_type=MESH)

    for copy in small_copies:
        copy.wait()
    side_rows = sbuf.shape[1]
    row_id = lax.broadcasted_iota(jnp.int32, (side_rows, seam), 0)
    for q in range(2):
        packed = jnp.where(row_id == rows, codes[0, 0].astype(F32), 0.0)
        packed = jnp.where(row_id == rows + 1, codes[0, 1].astype(F32), packed)
        packed = jnp.where(row_id == rows + 2, counts[0, 2 * s + q].astype(F32), packed)
        sbuf[q] = packed
        sbuf[q, 0:rows, :] = cour[2 * s + q]
    adj_copy.wait()
    for lev in range(levels):
        for r in range(rows):
            abuf[lev, r] = adj[pl.ds(lev * rows + r, species_dev, stride), :].astype(BF16)

    pl.semaphore_wait(barrier, 2 * levels - 1)

    sends = []

    def send(src, dst, send_sem, recv_sem, device):
        copy = pltpu.make_async_remote_copy(
            src_ref=src, dst_ref=dst, send_sem=send_sem, recv_sem=recv_sem,
            device_id=device, device_id_type=MESH,
        )
        copy.start()
        sends.append(copy)

    def owner(pair, lev):
        return (2 * pair + lax.rem(lev, 2), lev // 2)

    targets = ((1 - p, (2 * z + 1 - p, s), slot_own), (0, (2 * zn, s), slot_far), (1, (2 * zn + 1, s), slot_far))
    for i, (q, device, slot) in enumerate(targets):
        send(sbuf.at[q], side.at[slot], s_send.at[i], s_recv.at[slot], device)
    for d in range(levels):
        lev = lax.rem(own_level + d, levels)
        send(abuf.at[lev], gath.at[slot_far, s], a_send.at[0, d], a_recv.at[slot_far, s], owner(zn, lev))

    gath[slot_own, s] = abuf[own_level]
    side[slot_own] = sbuf[p]

    for copy in mat_copies:
        copy.wait()
    weights = power_weights()
    block = species // blocks
    row_s = lax.broadcasted_iota(jnp.int32, (species, species), 0)
    col_s = lax.broadcasted_iota(jnp.int32, (species, species), 1)
    jac_used = []
    for q in range(2):
        present = jnp.zeros((species, species), jnp.int32)
        for b in range(blocks):
            for e in range(blocks):
                inside = (
                    (row_s >= b * block) & (row_s < (b + 1) * block)
                    & (col_s >= e * block) & (col_s < (e + 1) * block)
                )
                present = jnp.where(inside, pattern[0, b, e, 2 * s + q], present)
        jac_used.append(jnp.where(present == 1, mats[2, q].astype(F32), 0.0).astype(BF16))
    both = [jnp.concatenate(split(dot(mats[0, q], mats[1, q])), axis=1) for q in range(2)]
    g = [dot(both[q], twice(jac_used[q])) for q in range(2)]
    both = [jnp.concatenate(split(g[q]), axis=1) for q in range(2)]
    acc = [weights[2] * g[q] + weights[3] * dot(both[q], twice(g[q].astype(BF16))) for q in range(2)]
    acc = [weights[1] * g[q] + dot(both[q], twice(acc[q].astype(BF16))) for q in range(2)]
    acc = [weights[0] * g[q] + dot(both[q], twice(acc[q].astype(BF16))) for q in range(2)]
    for q in range(2):
        ebuf[q] = jnp.transpose(acc[q]).astype(BF16)
    for i, (q, device, slot) in enumerate(targets):
        send(ebuf.at[q], emat.at[slot], e_send.at[i], e_recv.at[slot], device)
    for d in range(1, levels):
        lev = lax.rem(own_level + d, levels)
        send(abuf.at[lev], gath.at[slot_own, s], a_send.at[1, d], a_recv.at[slot_own, s], owner(z, lev))
    emat[slot_own] = ebuf[p]

    def arrived(dst, sem):
        pltpu.make_async_copy(dst, dst, sem).wait()

    for slot in (slot_other, 0, 3):
        arrived(side.at[slot], s_recv.at[slot])

    code_up1 = side[1, rows : rows + 1, :]
    code_down1 = side[1, rows + 1 : rows + 2, :]
    code_up2 = side[2, rows : rows + 1, :]
    flips = [code_down1, jnp.zeros_like(code_up1), code_up1, jnp.abs(code_up1 - code_up2)]
    row_y = lax.broadcasted_iota(jnp.int32, (seam, seam), 0)
    col_y = lax.broadcasted_iota(jnp.int32, (seam, seam), 1)
    eye = jnp.where(row_y == col_y, 1.0, 0.0)
    anti = jnp.where(row_y + col_y == seam - 1, 1.0, 0.0)
    perms = [(eye + (anti - eye) * flips[k]).astype(BF16) for k in range(4)]
    faces = []
    for k in range(4):
        block_k = side[k]
        if k != 1:
            hi = block_k.astype(BF16)
            rest = block_k - hi.astype(F32)
            mid = rest.astype(BF16)
            low = (rest - mid.astype(F32)).astype(BF16)
            block_k = dot(hi, perms[k]) + dot(mid, perms[k]) + dot(low, perms[k])
        for r in range(rows):
            faces.append(block_k[r : r + 1, :])

    lane = lax.broadcasted_iota(jnp.int32, (1, seam), 1).astype(F32)

    for k in (1, 2, 0, 3):
        if k == 1:
            arrived(emat.at[slot_other], e_recv.at[slot_other])
            for d in range(1, specs):
                src = lax.rem(s + d, specs)
                arrived(gath.at[slot_own, src], a_recv.at[slot_own, src])
            for src in range(specs):
                arrived(gath.at[slot_other, src], a_recv.at[slot_other, src])
        elif k != 2:
            arrived(emat.at[k], e_recv.at[k])
            for src in range(specs):
                arrived(gath.at[k, src], a_recv.at[k, src])
        field = [[gath[k, src, r] for src in range(specs)] for r in range(rows)]
        field = [jnp.concatenate(parts, axis=0) for parts in field]
        if k != 1:
            turned = dot(jnp.concatenate(field, axis=0), perms[k]).astype(BF16)
            field = [turned[r * species : (r + 1) * species] for r in range(rows)]
        chem = dot(emat[k], jnp.concatenate(field, axis=1))
        count = side[k, rows + 2 : rows + 3, :]
        place = lane + flips[k] * (seam - 1 - 2 * lane)
        for r in range(rows):
            active = (place + float(r * seam)) < count
            term = chem[:, r * seam : (r + 1) * seam]
            state[k * rows + r] = field[r].astype(F32) + jnp.where(active, term, 0.0)

    total = 4 * rows
    group = 16
    shape = (group, seam)

    def advect(who, within):
        at = pl.multiple_of(who * species_dev + within, group)
        a = [state[r, pl.ds(at, group), :] for r in range(total)]
        for step in range(1, NSUB + 1):
            new = list(a)
            for r in range(step, total - step):
                rising = jnp.maximum(faces[r], 0.0)
                falling = jnp.minimum(faces[r - 1], 0.0)
                new[r] = a[r] + rising * (a[r + 1] - a[r]) + falling * (a[r] - a[r - 1])
            a = new
        for r in range(rows):
            ret[0, who, r, within : within + group, :] = a[rows + r].astype(BF16)
        upper = jnp.concatenate([a[2 * rows + r] for r in range(rows)], axis=0).astype(BF16)
        upper = dot(upper, perms[2]).astype(BF16)
        for r in range(rows):
            ret[1, who, r, within : within + group, :] = upper[r * group : (r + 1) * group]

    for i in range(specs):
        who = lax.rem(s + 1 + i, specs)
        for within in range(0, species_dev, group):
            advect(who, within)
        for j in range(2):
            q = lax.rem(p + 1 + j, 2)
            if i < specs - 1 or j == 0:
                send(ret.at[q, who], out.at[own_level], r_send.at[2 * i + j], r_recv.at[own_level], (2 * z + q, who))
    own_copy = pltpu.make_async_copy(ret.at[p, s], out.at[own_level], own_sem)
    own_copy.start()
    for d in range(1, levels):
        lev = lax.rem(own_level + d, levels)
        arrived(out.at[lev], r_recv.at[lev])
    own_copy.wait()
    for copy in sends:
        copy.wait_send()


def unpack(levels, rows, part, packed, out):
    for lev in range(levels):
        for r in range(rows):
            out[pl.ds(lev * rows + r, part, levels * rows), :] = packed[lev, r].astype(F32)


def shards(tiles, specs, adjoint, section_first, section_second, jacobian, pattern, counts, courant, seam_codes):
    species_dev, levels, rows, seam = adjoint.shape
    species = jacobian.shape[2]
    assert levels == 2 * specs and tiles % 2 == 0 and rows >= NSUB
    side_rows = (rows + 3 + 7) // 8 * 8
    dma = pltpu.SemaphoreType.DMA
    out = pl.pallas_call(
        functools.partial(kernel, tiles, specs, levels, rows, species_dev, pattern.shape[2]),
        out_shape=jax.ShapeDtypeStruct((levels, rows, species_dev, seam), BF16),
        in_specs=[pl.BlockSpec(memory_space=pl.ANY)] * 8,
        out_specs=pl.BlockSpec(memory_space=pl.ANY),
        scratch_shapes=[
            pltpu.VMEM((species_dev * levels * rows, seam), F32),
            pltpu.VMEM((3, 2, species, species), BF16),
            pltpu.VMEM(courant.shape, F32),
            pltpu.SMEM((1,) + pattern.shape[2:] + (levels,), jnp.int32),
            pltpu.SMEM(counts.shape, jnp.int32),
            pltpu.SMEM(seam_codes.shape, jnp.int32),
            pltpu.VMEM((levels, rows, species_dev, seam), BF16),
            pltpu.VMEM((4, specs, rows, species_dev, seam), BF16),
            pltpu.VMEM((2, species, species), BF16),
            pltpu.VMEM((4, species, species), BF16),
            pltpu.VMEM((2, side_rows, seam), F32),
            pltpu.VMEM((4, side_rows, seam), F32),
            pltpu.VMEM((4 * rows, species, seam), F32),
            pltpu.VMEM((2, specs, rows, species_dev, seam), BF16),
            dma((8,)),
            dma(()),
            dma((2, levels)),
            dma((4, specs)),
            dma((3,)),
            dma((4,)),
            dma((3,)),
            dma((4,)),
            dma((levels,)),
            dma((levels,)),
        ],
        compiler_params=pltpu.CompilerParams(
            collective_id=0, has_side_effects=True, vmem_limit_bytes=60 * 1024 * 1024
        ),
    )(
        adjoint.reshape(species_dev * levels * rows, seam),
        section_first, section_second, jacobian, courant, jnp.transpose(pattern, (0, 2, 3, 1)), counts, seam_codes,
    )
    halves = 2
    part = species_dev // halves
    size = levels * rows
    final = pl.pallas_call(
        functools.partial(unpack, levels, rows, part),
        grid=(halves,),
        out_shape=jax.ShapeDtypeStruct((species_dev * size, seam), F32),
        in_specs=[pl.BlockSpec((levels, rows, part, seam), lambda i: (0, 0, i, 0))],
        out_specs=pl.BlockSpec((part * size, seam), lambda i: (i, 0)),
        cost_estimate=pl.CostEstimate(flops=0, bytes_accessed=6 * species_dev * size * seam, transcendentals=0),
    )(out)
    return final.reshape(species_dev, levels, rows, seam)


def solution(mesh):
    in_specs = (
        P("spec", None, "tile", None),
        P("tile", None, None, None),
        P("tile", None, None, None),
        P("tile", None, None, None),
        P("tile", None, None, None),
        P("tile", None),
        P(None, "tile", None),
        P("tile", None),
    )
    out_specs = P("spec", None, "tile", None)
    body = functools.partial(shards, mesh.shape["tile"], mesh.shape["spec"])
    return jax.shard_map(body, mesh=mesh, in_specs=in_specs, out_specs=out_specs, check_vma=False)
```

```python
import functools

import jax
import jax.numpy as jnp
from jax import lax
from jax.experimental import pallas as pl
from jax.experimental.pallas import tpu as pltpu
from jax.sharding import PartitionSpec as P

NSUB = 4

section_weights = (0.4, 0.3, 0.2, 0.1)
coupling = 0.5

MESH = pl.DeviceIdType.MESH
F32 = jnp.float32
BF16 = jnp.bfloat16


def power_weights():
    out = []
    for j in range(4):
        out.append((coupling**j) * sum(section_weights[j:]))
    return out


def dot(a, b):
    return jnp.dot(a, b, preferred_element_type=F32)


def split(x):
    hi = x.astype(BF16)
    return hi, (x - hi.astype(F32)).astype(BF16)


def twice(x):
    return jnp.concatenate([x, x], axis=0)


def kernel(
    tiles, specs, levels, rows, species_dev, blocks,
    adj_hbm, first_hbm, second_hbm, jac_hbm, cour_hbm, pattern_hbm, counts_hbm, codes_hbm,
    out,
    adj, mats, cour, pattern, counts, codes, abuf, gath, ebuf, emat, sbuf, side, state, ret,
    load_sem, own_sem, a_send, a_recv, e_send, e_recv, s_send, s_recv, r_send, r_recv,
):
    seam = adj.shape[1]
    species = specs * species_dev
    cells = rows * seam
    stride = levels * rows
    pairs = tiles // 2
    t = lax.axis_index("tile")
    s = lax.axis_index("spec")
    z = t // 2
    p = t - 2 * z
    zn = lax.rem(z + pairs - 1 + 2 * p, pairs)
    slot_own = 1 + p
    slot_other = 2 - p
    slot_far = 3 * (1 - p)
    own_level = 2 * s + p

    halves = 2
    part = species_dev // halves
    adj_copies = []
    for h in range(halves):
        span = pl.ds(h * part * stride, part * stride)
        copy = pltpu.make_async_copy(adj_hbm.at[span], adj.at[span], load_sem.at[h])
        copy.start()
        adj_copies.append(copy)
    small_copies = []
    for i, (ref, to) in enumerate(
        ((cour_hbm, cour), (counts_hbm, counts), (codes_hbm, codes), (pattern_hbm, pattern))
    ):
        copy = pltpu.make_async_copy(ref, to, load_sem.at[2 + i])
        copy.start()
        small_copies.append(copy)
    mat_copies = []
    for i, ref in enumerate((first_hbm, second_hbm, jac_hbm)):
        copy = pltpu.make_async_copy(ref.at[0, pl.ds(2 * s, 2)], mats.at[i], load_sem.at[6 + i])
        copy.start()
        mat_copies.append(copy)

    barrier = pltpu.get_barrier_semaphore()
    for d in range(1, levels):
        lev = lax.rem(own_level + d, levels)
        pl.semaphore_signal(barrier, inc=1, device_id=(2 * z + lax.rem(lev, 2), lev // 2), device_id_type=MESH)
    for src in range(specs):
        below = lax.rem(2 * z + tiles - 1, tiles)
        above = lax.rem(2 * z + 2, tiles)
        for q in (below, above):
            pl.semaphore_signal(barrier, inc=1, device_id=(q, src), device_id_type=MESH)

    for copy in small_copies:
        copy.wait()
    side_rows = sbuf.shape[1]
    row_id = lax.broadcasted_iota(jnp.int32, (side_rows, seam), 0)
    for q in range(2):
        packed = jnp.where(row_id == rows, codes[0, 0].astype(F32), 0.0)
        packed = jnp.where(row_id == rows + 1, codes[0, 1].astype(F32), packed)
        packed = jnp.where(row_id == rows + 2, counts[0, 2 * s + q].astype(F32), packed)
        sbuf[q] = packed
        sbuf[q, 0:rows, :] = cour[2 * s + q]
    for h in range(halves):
        adj_copies[h].wait()
        for lev in range(levels):
            for r in range(rows):
                start = h * part * stride + lev * rows + r
                abuf[lev, r, h * part : (h + 1) * part, :] = adj[pl.ds(start, part, stride), :].astype(BF16)

    pl.semaphore_wait(barrier, 2 * levels - 1)

    sends = []

    def send(src, dst, send_sem, recv_sem, device):
        copy = pltpu.make_async_remote_copy(
            src_ref=src, dst_ref=dst, send_sem=send_sem, recv_sem=recv_sem,
            device_id=device, device_id_type=MESH,
        )
        copy.start()
        sends.append(copy)

    def owner(pair, lev):
        return (2 * pair + lax.rem(lev, 2), lev // 2)

    targets = ((1 - p, (2 * z + 1 - p, s), slot_own), (0, (2 * zn, s), slot_far), (1, (2 * zn + 1, s), slot_far))
    for i, (q, device, slot) in enumerate(targets):
        send(sbuf.at[q], side.at[slot], s_send.at[i], s_recv.at[slot], device)
    for d in range(levels):
        lev = lax.rem(own_level + d, levels)
        send(abuf.at[lev], gath.at[slot_far, s], a_send.at[0, d], a_recv.at[slot_far, s], owner(zn, lev))

    for d in range(1, levels):
        lev = lax.rem(own_level + d, levels)
        send(abuf.at[lev], gath.at[slot_own, s], a_send.at[1, d], a_recv.at[slot_own, s], owner(z, lev))
    gath[slot_own, s] = abuf[own_level]
    side[slot_own] = sbuf[p]

    for copy in mat_copies:
        copy.wait()
    weights = power_weights()
    block = species // blocks
    row_s = lax.broadcasted_iota(jnp.int32, (species, species), 0)
    col_s = lax.broadcasted_iota(jnp.int32, (species, species), 1)
    jac_used = []
    for q in range(2):
        present = jnp.zeros((species, species), jnp.int32)
        for b in range(blocks):
            for e in range(blocks):
                inside = (
                    (row_s >= b * block) & (row_s < (b + 1) * block)
                    & (col_s >= e * block) & (col_s < (e + 1) * block)
                )
                present = jnp.where(inside, pattern[0, b, e, 2 * s + q], present)
        jac_used.append(jnp.where(present == 1, mats[2, q].astype(F32), 0.0).astype(BF16))
    both = [jnp.concatenate(split(dot(mats[0, q], mats[1, q])), axis=1) for q in range(2)]
    g = [dot(both[q], twice(jac_used[q])) for q in range(2)]
    both = [jnp.concatenate(split(g[q]), axis=1) for q in range(2)]
    acc = [weights[2] * g[q] + weights[3] * dot(both[q], twice(g[q].astype(BF16))) for q in range(2)]
    acc = [weights[1] * g[q] + dot(both[q], twice(acc[q].astype(BF16))) for q in range(2)]
    acc = [weights[0] * g[q] + dot(both[q], twice(acc[q].astype(BF16))) for q in range(2)]
    for q in range(2):
        ebuf[q] = jnp.transpose(acc[q]).astype(BF16)
    for i, (q, device, slot) in enumerate(targets):
        send(ebuf.at[q], emat.at[slot], e_send.at[i], e_recv.at[slot], device)
    emat[slot_own] = ebuf[p]

    def arrived(dst, sem):
        pltpu.make_async_copy(dst, dst, sem).wait()

    for slot in (slot_other, 0, 3):
        arrived(side.at[slot], s_recv.at[slot])

    code_up1 = side[1, rows : rows + 1, :]
    code_down1 = side[1, rows + 1 : rows + 2, :]
    code_up2 = side[2, rows : rows + 1, :]
    flips = [code_down1, jnp.zeros_like(code_up1), code_up1, jnp.abs(code_up1 - code_up2)]
    row_y = lax.broadcasted_iota(jnp.int32, (seam, seam), 0)
    col_y = lax.broadcasted_iota(jnp.int32, (seam, seam), 1)
    eye = jnp.where(row_y == col_y, 1.0, 0.0)
    anti = jnp.where(row_y + col_y == seam - 1, 1.0, 0.0)
    perms = [(eye + (anti - eye) * flips[k]).astype(BF16) for k in range(4)]
    faces = []
    for k in range(4):
        block_k = side[k]
        if k != 1:
            hi = block_k.astype(BF16)
            rest = block_k - hi.astype(F32)
            mid = rest.astype(BF16)
            low = (rest - mid.astype(F32)).astype(BF16)
            block_k = dot(hi, perms[k]) + dot(mid, perms[k]) + dot(low, perms[k])
        for r in range(rows):
            faces.append(block_k[r : r + 1, :])

    lane = lax.broadcasted_iota(jnp.int32, (1, seam), 1).astype(F32)

    for k in (1, 2, 0, 3):
        if k == 1:
            arrived(emat.at[slot_other], e_recv.at[slot_other])
            for d in range(1, specs):
                src = lax.rem(s + d, specs)
                arrived(gath.at[slot_own, src], a_recv.at[slot_own, src])
            for src in range(specs):
                arrived(gath.at[slot_other, src], a_recv.at[slot_other, src])
        elif k != 2:
            arrived(emat.at[k], e_recv.at[k])
            for src in range(specs):
                arrived(gath.at[k, src], a_recv.at[k, src])
        field = [[gath[k, src, r] for src in range(specs)] for r in range(rows)]
        field = [jnp.concatenate(parts, axis=0) for parts in field]
        if k != 1:
            turned = dot(jnp.concatenate(field, axis=0), perms[k]).astype(BF16)
            field = [turned[r * species : (r + 1) * species] for r in range(rows)]
        chem = dot(emat[k], jnp.concatenate(field, axis=1))
        count = side[k, rows + 2 : rows + 3, :]
        place = lane + flips[k] * (seam - 1 - 2 * lane)
        for r in range(rows):
            active = (place + float(r * seam)) < count
            term = chem[:, r * seam : (r + 1) * seam]
            state[k * rows + r] = field[r].astype(F32) + jnp.where(active, term, 0.0)

    total = 4 * rows
    group = 16
    shape = (group, seam)

    def advect(who, within):
        at = pl.multiple_of(who * species_dev + within, group)
        a = [state[r, pl.ds(at, group), :] for r in range(total)]
        for step in range(1, NSUB + 1):
            new = list(a)
            for r in range(step, total - step):
                rising = jnp.maximum(faces[r], 0.0)
                falling = jnp.minimum(faces[r - 1], 0.0)
                new[r] = a[r] + rising * (a[r + 1] - a[r]) + falling * (a[r] - a[r - 1])
            a = new
        for r in range(rows):
            ret[0, who, r, within : within + group, :] = a[rows + r].astype(BF16)
        upper = jnp.concatenate([a[2 * rows + r] for r in range(rows)], axis=0).astype(BF16)
        upper = dot(upper, perms[2]).astype(BF16)
        for r in range(rows):
            ret[1, who, r, within : within + group, :] = upper[r * group : (r + 1) * group]

    for i in range(specs):
        who = lax.rem(s + 1 + i, specs)
        for within in range(0, species_dev, group):
            advect(who, within)
        for j in range(2):
            q = lax.rem(p + 1 + j, 2)
            if i < specs - 1 or j == 0:
                send(ret.at[q, who], out.at[own_level], r_send.at[2 * i + j], r_recv.at[own_level], (2 * z + q, who))
    own_copy = pltpu.make_async_copy(ret.at[p, s], out.at[own_level], own_sem)
    own_copy.start()
    for d in range(1, levels):
        lev = lax.rem(own_level + d, levels)
        arrived(out.at[lev], r_recv.at[lev])
    own_copy.wait()
    for copy in sends:
        copy.wait_send()


def unpack(packed_hbm, out_hbm, packed, out, in_sem, out_sem):
    levels, rows, species_dev, seam = packed.shape
    halves = 2
    part = species_dev // halves
    stride = levels * rows
    loads = []
    for h in range(halves):
        span = pl.ds(h * part, part)
        copy = pltpu.make_async_copy(packed_hbm.at[:, :, span], packed.at[:, :, span], in_sem.at[h])
        copy.start()
        loads.append(copy)
    stores = []
    for h in range(halves):
        loads[h].wait()
        for lev in range(levels):
            for r in range(rows):
                start = h * part * stride + lev * rows + r
                out[pl.ds(start, part, stride), :] = packed[lev, r, h * part : (h + 1) * part, :].astype(F32)
        span = pl.ds(h * part * stride, part * stride)
        copy = pltpu.make_async_copy(out.at[span], out_hbm.at[span], out_sem.at[h])
        copy.start()
        stores.append(copy)
    for copy in stores:
        copy.wait()


def shards(tiles, specs, adjoint, section_first, section_second, jacobian, pattern, counts, courant, seam_codes):
    species_dev, levels, rows, seam = adjoint.shape
    species = jacobian.shape[2]
    assert levels == 2 * specs and tiles % 2 == 0 and rows >= NSUB
    side_rows = (rows + 3 + 7) // 8 * 8
    dma = pltpu.SemaphoreType.DMA
    out = pl.pallas_call(
        functools.partial(kernel, tiles, specs, levels, rows, species_dev, pattern.shape[2]),
        out_shape=jax.ShapeDtypeStruct((levels, rows, species_dev, seam), BF16),
        in_specs=[pl.BlockSpec(memory_space=pl.ANY)] * 8,
        out_specs=pl.BlockSpec(memory_space=pl.ANY),
        scratch_shapes=[
            pltpu.VMEM((species_dev * levels * rows, seam), F32),
            pltpu.VMEM((3, 2, species, species), BF16),
            pltpu.VMEM(courant.shape, F32),
            pltpu.SMEM((1,) + pattern.shape[2:] + (levels,), jnp.int32),
            pltpu.SMEM(counts.shape, jnp.int32),
            pltpu.SMEM(seam_codes.shape, jnp.int32),
            pltpu.VMEM((levels, rows, species_dev, seam), BF16),
            pltpu.VMEM((4, specs, rows, species_dev, seam), BF16),
            pltpu.VMEM((2, species, species), BF16),
            pltpu.VMEM((4, species, species), BF16),
            pltpu.VMEM((2, side_rows, seam), F32),
            pltpu.VMEM((4, side_rows, seam), F32),
            pltpu.VMEM((4 * rows, species, seam), F32),
            pltpu.VMEM((2, specs, rows, species_dev, seam), BF16),
            dma((9,)),
            dma(()),
            dma((2, levels)),
            dma((4, specs)),
            dma((3,)),
            dma((4,)),
            dma((3,)),
            dma((4,)),
            dma((levels,)),
            dma((levels,)),
        ],
        compiler_params=pltpu.CompilerParams(
            collective_id=0, has_side_effects=True, vmem_limit_bytes=60 * 1024 * 1024
        ),
    )(
        adjoint.reshape(species_dev * levels * rows, seam),
        section_first, section_second, jacobian, courant, jnp.transpose(pattern, (0, 2, 3, 1)), counts, seam_codes,
    )
    size = species_dev * levels * rows
    final = pl.pallas_call(
        unpack,
        out_shape=jax.ShapeDtypeStruct((size, seam), F32),
        in_specs=[pl.BlockSpec(memory_space=pl.ANY)],
        out_specs=pl.BlockSpec(memory_space=pl.ANY),
        scratch_shapes=[
            pltpu.VMEM((levels, rows, species_dev, seam), BF16),
            pltpu.VMEM((size, seam), F32),
            dma((2,)),
            dma((2,)),
        ],
        compiler_params=pltpu.CompilerParams(vmem_limit_bytes=60 * 1024 * 1024),
        cost_estimate=pl.CostEstimate(flops=0, bytes_accessed=6 * size * seam, transcendentals=0),
    )(out)
    return final.reshape(species_dev, levels, rows, seam)


def solution(mesh):
    in_specs = (
        P("spec", None, "tile", None),
        P("tile", None, None, None),
        P("tile", None, None, None),
        P("tile", None, None, None),
        P("tile", None, None, None),
        P("tile", None),
        P(None, "tile", None),
        P("tile", None),
    )
    out_specs = P("spec", None, "tile", None)
    body = functools.partial(shards, mesh.shape["tile"], mesh.shape["spec"])
    return jax.shard_map(body, mesh=mesh, in_specs=in_specs, out_specs=out_specs, check_vma=False)
```

```python
import functools

import jax
import jax.numpy as jnp
from jax import lax
from jax.experimental import pallas as pl
from jax.experimental.pallas import tpu as pltpu
from jax.sharding import PartitionSpec as P

NSUB = 4

section_weights = (0.4, 0.3, 0.2, 0.1)
coupling = 0.5

MESH = pl.DeviceIdType.MESH
F32 = jnp.float32
BF16 = jnp.bfloat16


def padded_pitch(count):
    tiles = (count + 7) // 8
    return 8 * (tiles + 1 - tiles % 2)


def power_weights():
    out = []
    for j in range(4):
        out.append((coupling**j) * sum(section_weights[j:]))
    return out


def dot(a, b):
    return jnp.dot(a, b, preferred_element_type=F32)


def split(x):
    hi = x.astype(BF16)
    return hi, (x - hi.astype(F32)).astype(BF16)


def twice(x):
    return jnp.concatenate([x, x], axis=0)


def kernel(
    tiles, specs, levels, rows, species_dev, blocks,
    adj_hbm, first_hbm, second_hbm, jac_hbm, cour_hbm, pattern_hbm, counts_hbm, codes_hbm,
    out,
    adj, mats, cour, pattern, counts, codes, abuf, gath, ebuf, emat, sbuf, side, state, ret,
    load_sem, own_sem, a_send, a_recv, e_send, e_recv, s_send, s_recv, r_send, r_recv,
):
    seam = adj.shape[1]
    species = specs * species_dev
    cells = rows * seam
    stride = levels * rows
    pitch = padded_pitch(stride)
    pairs = tiles // 2
    t = lax.axis_index("tile")
    s = lax.axis_index("spec")
    z = t // 2
    p = t - 2 * z
    zn = lax.rem(z + pairs - 1 + 2 * p, pairs)
    slot_own = 1 + p
    slot_other = 2 - p
    slot_far = 3 * (1 - p)
    own_level = 2 * s + p

    halves = 2
    part = species_dev // halves
    adj_copies = []
    for h in range(halves):
        span = pl.ds(h * part, part)
        copy = pltpu.make_async_copy(
            adj_hbm.at[span], adj.reshape(species_dev, pitch, seam).at[span, pl.ds(0, stride)], load_sem.at[h]
        )
        copy.start()
        adj_copies.append(copy)
    small_copies = []
    for i, (ref, to) in enumerate(
        ((cour_hbm, cour), (counts_hbm, counts), (codes_hbm, codes), (pattern_hbm, pattern))
    ):
        copy = pltpu.make_async_copy(ref, to, load_sem.at[2 + i])
        copy.start()
        small_copies.append(copy)
    mat_copies = []
    for i, ref in enumerate((first_hbm, second_hbm, jac_hbm)):
        copy = pltpu.make_async_copy(ref.at[0, pl.ds(2 * s, 2)], mats.at[i], load_sem.at[6 + i])
        copy.start()
        mat_copies.append(copy)

    barrier = pltpu.get_barrier_semaphore()
    for d in range(1, levels):
        lev = lax.rem(own_level + d, levels)
        pl.semaphore_signal(barrier, inc=1, device_id=(2 * z + lax.rem(lev, 2), lev // 2), device_id_type=MESH)
    for src in range(specs):
        below = lax.rem(2 * z + tiles - 1, tiles)
        above = lax.rem(2 * z + 2, tiles)
        for q in (below, above):
            pl.semaphore_signal(barrier, inc=1, device_id=(q, src), device_id_type=MESH)

    for copy in small_copies:
        copy.wait()
    side_rows = sbuf.shape[1]
    row_id = lax.broadcasted_iota(jnp.int32, (side_rows, seam), 0)
    for q in range(2):
        packed = jnp.where(row_id == rows, codes[0, 0].astype(F32), 0.0)
        packed = jnp.where(row_id == rows + 1, codes[0, 1].astype(F32), packed)
        packed = jnp.where(row_id == rows + 2, counts[0, 2 * s + q].astype(F32), packed)
        sbuf[q] = packed
        sbuf[q, 0:rows, :] = cour[2 * s + q]
    for h in range(halves):
        adj_copies[h].wait()
        for lev in range(levels):
            for r in range(rows):
                start = h * part * pitch + lev * rows + r
                abuf[lev, r, h * part : (h + 1) * part, :] = adj[pl.ds(start, part, pitch), :].astype(BF16)

    pl.semaphore_wait(barrier, 2 * levels - 1)

    sends = []

    def send(src, dst, send_sem, recv_sem, device):
        copy = pltpu.make_async_remote_copy(
            src_ref=src, dst_ref=dst, send_sem=send_sem, recv_sem=recv_sem,
            device_id=device, device_id_type=MESH,
        )
        copy.start()
        sends.append(copy)

    def owner(pair, lev):
        return (2 * pair + lax.rem(lev, 2), lev // 2)

    targets = ((1 - p, (2 * z + 1 - p, s), slot_own), (0, (2 * zn, s), slot_far), (1, (2 * zn + 1, s), slot_far))
    for i, (q, device, slot) in enumerate(targets):
        send(sbuf.at[q], side.at[slot], s_send.at[i], s_recv.at[slot], device)
    for d in range(levels):
        lev = lax.rem(own_level + d, levels)
        send(abuf.at[lev], gath.at[slot_far, s], a_send.at[0, d], a_recv.at[slot_far, s], owner(zn, lev))

    for d in range(1, levels):
        lev = lax.rem(own_level + d, levels)
        send(abuf.at[lev], gath.at[slot_own, s], a_send.at[1, d], a_recv.at[slot_own, s], owner(z, lev))
    gath[slot_own, s] = abuf[own_level]
    side[slot_own] = sbuf[p]

    for copy in mat_copies:
        copy.wait()
    weights = power_weights()
    block = species // blocks
    row_s = lax.broadcasted_iota(jnp.int32, (species, species), 0)
    col_s = lax.broadcasted_iota(jnp.int32, (species, species), 1)
    jac_used = []
    for q in range(2):
        present = jnp.zeros((species, species), jnp.int32)
        for b in range(blocks):
            for e in range(blocks):
                inside = (
                    (row_s >= b * block) & (row_s < (b + 1) * block)
                    & (col_s >= e * block) & (col_s < (e + 1) * block)
                )
                present = jnp.where(inside, pattern[0, b, e, 2 * s + q], present)
        jac_used.append(jnp.where(present == 1, mats[2, q].astype(F32), 0.0).astype(BF16))
    both = [jnp.concatenate(split(dot(mats[0, q], mats[1, q])), axis=1) for q in range(2)]
    g = [dot(both[q], twice(jac_used[q])) for q in range(2)]
    both = [jnp.concatenate(split(g[q]), axis=1) for q in range(2)]
    acc = [weights[2] * g[q] + weights[3] * dot(both[q], twice(g[q].astype(BF16))) for q in range(2)]
    acc = [weights[1] * g[q] + dot(both[q], twice(acc[q].astype(BF16))) for q in range(2)]
    acc = [weights[0] * g[q] + dot(both[q], twice(acc[q].astype(BF16))) for q in range(2)]
    for q in range(2):
        ebuf[q] = jnp.transpose(acc[q]).astype(BF16)
    for i, (q, device, slot) in enumerate(targets):
        send(ebuf.at[q], emat.at[slot], e_send.at[i], e_recv.at[slot], device)
    emat[slot_own] = ebuf[p]

    def arrived(dst, sem):
        pltpu.make_async_copy(dst, dst, sem).wait()

    for slot in (slot_other, 0, 3):
        arrived(side.at[slot], s_recv.at[slot])

    code_up1 = side[1, rows : rows + 1, :]
    code_down1 = side[1, rows + 1 : rows + 2, :]
    code_up2 = side[2, rows : rows + 1, :]
    flips = [code_down1, jnp.zeros_like(code_up1), code_up1, jnp.abs(code_up1 - code_up2)]
    row_y = lax.broadcasted_iota(jnp.int32, (seam, seam), 0)
    col_y = lax.broadcasted_iota(jnp.int32, (seam, seam), 1)
    eye = jnp.where(row_y == col_y, 1.0, 0.0)
    anti = jnp.where(row_y + col_y == seam - 1, 1.0, 0.0)
    perms = [(eye + (anti - eye) * flips[k]).astype(BF16) for k in range(4)]
    faces = []
    for k in range(4):
        block_k = side[k]
        if k != 1:
            hi = block_k.astype(BF16)
            rest = block_k - hi.astype(F32)
            mid = rest.astype(BF16)
            low = (rest - mid.astype(F32)).astype(BF16)
            block_k = dot(hi, perms[k]) + dot(mid, perms[k]) + dot(low, perms[k])
        for r in range(rows):
            faces.append(block_k[r : r + 1, :])

    lane = lax.broadcasted_iota(jnp.int32, (1, seam), 1).astype(F32)

    for k in (1, 2, 0, 3):
        if k == 1:
            arrived(emat.at[slot_other], e_recv.at[slot_other])
            for d in range(1, specs):
                src = lax.rem(s + d, specs)
                arrived(gath.at[slot_own, src], a_recv.at[slot_own, src])
            for src in range(specs):
                arrived(gath.at[slot_other, src], a_recv.at[slot_other, src])
        elif k != 2:
            arrived(emat.at[k], e_recv.at[k])
            for src in range(specs):
                arrived(gath.at[k, src], a_recv.at[k, src])
        field = [[gath[k, src, r] for src in range(specs)] for r in range(rows)]
        field = [jnp.concatenate(parts, axis=0) for parts in field]
        if k != 1:
            turned = dot(jnp.concatenate(field, axis=0), perms[k]).astype(BF16)
            field = [turned[r * species : (r + 1) * species] for r in range(rows)]
        chem = dot(emat[k], jnp.concatenate(field, axis=1))
        count = side[k, rows + 2 : rows + 3, :]
        place = lane + flips[k] * (seam - 1 - 2 * lane)
        for r in range(rows):
            active = (place + float(r * seam)) < count
            term = chem[:, r * seam : (r + 1) * seam]
            state[k * rows + r] = field[r].astype(F32) + jnp.where(active, term, 0.0)

    total = 4 * rows
    group = 16
    shape = (group, seam)

    def advect(who, within):
        at = pl.multiple_of(who * species_dev + within, group)
        a = [state[r, pl.ds(at, group), :] for r in range(total)]
        for step in range(1, NSUB + 1):
            new = list(a)
            for r in range(step, total - step):
                rising = jnp.maximum(faces[r], 0.0)
                falling = jnp.minimum(faces[r - 1], 0.0)
                new[r] = a[r] + rising * (a[r + 1] - a[r]) + falling * (a[r] - a[r - 1])
            a = new
        for r in range(rows):
            ret[0, who, r, within : within + group, :] = a[rows + r].astype(BF16)
        upper = jnp.concatenate([a[2 * rows + r] for r in range(rows)], axis=0).astype(BF16)
        upper = dot(upper, perms[2]).astype(BF16)
        for r in range(rows):
            ret[1, who, r, within : within + group, :] = upper[r * group : (r + 1) * group]

    for i in range(specs):
        who = lax.rem(s + 1 + i, specs)
        for within in range(0, species_dev, group):
            advect(who, within)
        for j in range(2):
            q = lax.rem(p + 1 + j, 2)
            if i < specs - 1 or j == 0:
                send(ret.at[q, who], out.at[own_level], r_send.at[2 * i + j], r_recv.at[own_level], (2 * z + q, who))
    own_copy = pltpu.make_async_copy(ret.at[p, s], out.at[own_level], own_sem)
    own_copy.start()
    for d in range(1, levels):
        lev = lax.rem(own_level + d, levels)
        arrived(out.at[lev], r_recv.at[lev])
    own_copy.wait()
    for copy in sends:
        copy.wait_send()


def unpack(packed_hbm, out_hbm, packed, out, in_sem, out_sem):
    levels, rows, species_dev, seam = packed.shape
    halves = 2
    part = species_dev // halves
    stride = levels * rows
    pitch = padded_pitch(stride)
    loads = []
    for h in range(halves):
        span = pl.ds(h * part, part)
        copy = pltpu.make_async_copy(packed_hbm.at[:, :, span], packed.at[:, :, span], in_sem.at[h])
        copy.start()
        loads.append(copy)
    stores = []
    for h in range(halves):
        loads[h].wait()
        for lev in range(levels):
            for r in range(rows):
                start = h * part * pitch + lev * rows + r
                out[pl.ds(start, part, pitch), :] = packed[lev, r, h * part : (h + 1) * part, :].astype(F32)
        span = pl.ds(h * part, part)
        copy = pltpu.make_async_copy(
            out.reshape(species_dev, pitch, seam).at[span, pl.ds(0, stride)], out_hbm.at[span], out_sem.at[h]
        )
        copy.start()
        stores.append(copy)
    for copy in stores:
        copy.wait()


def shards(tiles, specs, adjoint, section_first, section_second, jacobian, pattern, counts, courant, seam_codes):
    species_dev, levels, rows, seam = adjoint.shape
    species = jacobian.shape[2]
    assert levels == 2 * specs and tiles % 2 == 0 and rows >= NSUB
    side_rows = (rows + 3 + 7) // 8 * 8
    dma = pltpu.SemaphoreType.DMA
    out = pl.pallas_call(
        functools.partial(kernel, tiles, specs, levels, rows, species_dev, pattern.shape[2]),
        out_shape=jax.ShapeDtypeStruct((levels, rows, species_dev, seam), BF16),
        in_specs=[pl.BlockSpec(memory_space=pl.ANY)] * 8,
        out_specs=pl.BlockSpec(memory_space=pl.ANY),
        scratch_shapes=[
            pltpu.VMEM((species_dev * padded_pitch(levels * rows), seam), F32),
            pltpu.VMEM((3, 2, species, species), BF16),
            pltpu.VMEM(courant.shape, F32),
            pltpu.SMEM((1,) + pattern.shape[2:] + (levels,), jnp.int32),
            pltpu.SMEM(counts.shape, jnp.int32),
            pltpu.SMEM(seam_codes.shape, jnp.int32),
            pltpu.VMEM((levels, rows, species_dev, seam), BF16),
            pltpu.VMEM((4, specs, rows, species_dev, seam), BF16),
            pltpu.VMEM((2, species, species), BF16),
            pltpu.VMEM((4, species, species), BF16),
            pltpu.VMEM((2, side_rows, seam), F32),
            pltpu.VMEM((4, side_rows, seam), F32),
            pltpu.VMEM((4 * rows, species, seam), F32),
            pltpu.VMEM((2, specs, rows, species_dev, seam), BF16),
            dma((9,)),
            dma(()),
            dma((2, levels)),
            dma((4, specs)),
            dma((3,)),
            dma((4,)),
            dma((3,)),
            dma((4,)),
            dma((levels,)),
            dma((levels,)),
        ],
        compiler_params=pltpu.CompilerParams(
            collective_id=0, has_side_effects=True, vmem_limit_bytes=60 * 1024 * 1024
        ),
    )(
        adjoint.reshape(species_dev, levels * rows, seam),
        section_first, section_second, jacobian, courant, jnp.transpose(pattern, (0, 2, 3, 1)), counts, seam_codes,
    )
    size = species_dev * levels * rows
    final = pl.pallas_call(
        unpack,
        out_shape=jax.ShapeDtypeStruct((species_dev, levels * rows, seam), F32),
        in_specs=[pl.BlockSpec(memory_space=pl.ANY)],
        out_specs=pl.BlockSpec(memory_space=pl.ANY),
        scratch_shapes=[
            pltpu.VMEM((levels, rows, species_dev, seam), BF16),
            pltpu.VMEM((species_dev * padded_pitch(levels * rows), seam), F32),
            dma((2,)),
            dma((2,)),
        ],
        compiler_params=pltpu.CompilerParams(vmem_limit_bytes=60 * 1024 * 1024),
        cost_estimate=pl.CostEstimate(flops=0, bytes_accessed=6 * size * seam, transcendentals=0),
    )(out)
    return final.reshape(species_dev, levels, rows, seam)


def solution(mesh):
    in_specs = (
        P("spec", None, "tile", None),
        P("tile", None, None, None),
        P("tile", None, None, None),
        P("tile", None, None, None),
        P("tile", None, None, None),
        P("tile", None),
        P(None, "tile", None),
        P("tile", None),
    )
    out_specs = P("spec", None, "tile", None)
    body = functools.partial(shards, mesh.shape["tile"], mesh.shape["spec"])
    return jax.shard_map(body, mesh=mesh, in_specs=in_specs, out_specs=out_specs, check_vma=False)
```

```python
import functools

import jax
import jax.numpy as jnp
from jax import lax
from jax.experimental import pallas as pl
from jax.experimental.pallas import tpu as pltpu
from jax.sharding import PartitionSpec as P

NSUB = 4

section_weights = (0.4, 0.3, 0.2, 0.1)
coupling = 0.5

MESH = pl.DeviceIdType.MESH
F32 = jnp.float32
BF16 = jnp.bfloat16


def padded_pitch(count):
    tiles = (count + 7) // 8
    return 8 * (tiles + 1 - tiles % 2)


def power_weights():
    out = []
    for j in range(4):
        out.append((coupling**j) * sum(section_weights[j:]))
    return out


def dot(a, b):
    return jnp.dot(a, b, preferred_element_type=F32)


def split(x):
    hi = x.astype(BF16)
    return hi, (x - hi.astype(F32)).astype(BF16)


def twice(x):
    return jnp.concatenate([x, x], axis=0)


def kernel(
    tiles, specs, levels, rows, species_dev, blocks,
    adj_hbm, first_hbm, second_hbm, jac_hbm, cour_hbm, pattern_hbm, counts_hbm, codes_hbm,
    out,
    adj, mats, cour, pattern, counts, codes, abuf, gath, ebuf, emat, sbuf, side, state, ret,
    load_sem, own_sem, a_send, a_recv, e_send, e_recv, s_send, s_recv, r_send, r_recv,
):
    seam = adj.shape[1]
    species = specs * species_dev
    cells = rows * seam
    stride = levels * rows
    pitch = padded_pitch(stride)
    pairs = tiles // 2
    t = lax.axis_index("tile")
    s = lax.axis_index("spec")
    z = t // 2
    p = t - 2 * z
    zn = lax.rem(z + pairs - 1 + 2 * p, pairs)
    slot_own = 1 + p
    slot_other = 2 - p
    slot_far = 3 * (1 - p)
    own_level = 2 * s + p

    halves = 2
    part = species_dev // halves
    adj_copies = []
    for h in range(halves):
        span = pl.ds(h * part, part)
        copy = pltpu.make_async_copy(
            adj_hbm.at[span], adj.reshape(species_dev, pitch, seam).at[span, pl.ds(0, stride)], load_sem.at[h]
        )
        copy.start()
        adj_copies.append(copy)
    small_copies = []
    for i, (ref, to) in enumerate(
        ((cour_hbm, cour), (counts_hbm, counts), (codes_hbm, codes), (pattern_hbm, pattern))
    ):
        copy = pltpu.make_async_copy(ref, to, load_sem.at[2 + i])
        copy.start()
        small_copies.append(copy)
    mat_copies = []
    for i, ref in enumerate((first_hbm, second_hbm, jac_hbm)):
        copy = pltpu.make_async_copy(ref.at[0, pl.ds(2 * s, 2)], mats.at[i], load_sem.at[6 + i])
        copy.start()
        mat_copies.append(copy)

    barrier = pltpu.get_barrier_semaphore()
    for d in range(1, levels):
        lev = lax.rem(own_level + d, levels)
        pl.semaphore_signal(barrier, inc=1, device_id=(2 * z + lax.rem(lev, 2), lev // 2), device_id_type=MESH)
    for src in range(specs):
        below = lax.rem(2 * z + tiles - 1, tiles)
        above = lax.rem(2 * z + 2, tiles)
        for q in (below, above):
            pl.semaphore_signal(barrier, inc=1, device_id=(q, src), device_id_type=MESH)

    for copy in small_copies:
        copy.wait()
    side_rows = sbuf.shape[1]
    row_id = lax.broadcasted_iota(jnp.int32, (side_rows, seam), 0)
    for q in range(2):
        packed = jnp.where(row_id == rows, codes[0, 0].astype(F32), 0.0)
        packed = jnp.where(row_id == rows + 1, codes[0, 1].astype(F32), packed)
        packed = jnp.where(row_id == rows + 2, counts[0, 2 * s + q].astype(F32), packed)
        sbuf[q] = packed
        sbuf[q, 0:rows, :] = cour[2 * s + q]
    for h in range(halves):
        adj_copies[h].wait()
        for lev in range(levels):
            for r in range(rows):
                start = h * part * pitch + lev * rows + r
                abuf[lev, r, h * part : (h + 1) * part, :] = adj[pl.ds(start, part, pitch), :].astype(BF16)

    pl.semaphore_wait(barrier, 2 * levels - 1)

    sends = []

    def send(src, dst, send_sem, recv_sem, device):
        copy = pltpu.make_async_remote_copy(
            src_ref=src, dst_ref=dst, send_sem=send_sem, recv_sem=recv_sem,
            device_id=device, device_id_type=MESH,
        )
        copy.start()
        sends.append(copy)

    def owner(pair, lev):
        return (2 * pair + lax.rem(lev, 2), lev // 2)

    targets = ((1 - p, (2 * z + 1 - p, s), slot_own), (0, (2 * zn, s), slot_far), (1, (2 * zn + 1, s), slot_far))
    for i, (q, device, slot) in enumerate(targets):
        send(sbuf.at[q], side.at[slot], s_send.at[i], s_recv.at[slot], device)
    for d in range(levels):
        lev = lax.rem(own_level + d, levels)
        send(abuf.at[lev], gath.at[slot_far, s], a_send.at[0, d], a_recv.at[slot_far, s], owner(zn, lev))

    for d in range(1, levels):
        lev = lax.rem(own_level + d, levels)
        send(abuf.at[lev], gath.at[slot_own, s], a_send.at[1, d], a_recv.at[slot_own, s], owner(z, lev))
    gath[slot_own, s] = abuf[own_level]
    side[slot_own] = sbuf[p]

    for copy in mat_copies:
        copy.wait()
    weights = power_weights()
    block = species // blocks
    row_s = lax.broadcasted_iota(jnp.int32, (species, species), 0)
    col_s = lax.broadcasted_iota(jnp.int32, (species, species), 1)
    jac_used = []
    for q in range(2):
        present = jnp.zeros((species, species), jnp.int32)
        for b in range(blocks):
            for e in range(blocks):
                inside = (
                    (row_s >= b * block) & (row_s < (b + 1) * block)
                    & (col_s >= e * block) & (col_s < (e + 1) * block)
                )
                present = jnp.where(inside, pattern[0, b, e, 2 * s + q], present)
        jac_used.append(jnp.where(present == 1, mats[2, q].astype(F32), 0.0).astype(BF16))
    both = [jnp.concatenate(split(dot(mats[0, q], mats[1, q])), axis=1) for q in range(2)]
    g = [dot(both[q], twice(jac_used[q])) for q in range(2)]
    both = [jnp.concatenate(split(g[q]), axis=1) for q in range(2)]
    acc = [weights[2] * g[q] + weights[3] * dot(both[q], twice(g[q].astype(BF16))) for q in range(2)]
    acc = [weights[1] * g[q] + dot(both[q], twice(acc[q].astype(BF16))) for q in range(2)]
    acc = [weights[0] * g[q] + dot(both[q], twice(acc[q].astype(BF16))) for q in range(2)]
    for q in range(2):
        ebuf[q] = jnp.transpose(acc[q]).astype(BF16)
    for i, (q, device, slot) in enumerate(targets):
        send(ebuf.at[q], emat.at[slot], e_send.at[i], e_recv.at[slot], device)
    emat[slot_own] = ebuf[p]

    def arrived(dst, sem):
        pltpu.make_async_copy(dst, dst, sem).wait()

    for slot in (slot_other, 0, 3):
        arrived(side.at[slot], s_recv.at[slot])

    code_up1 = side[1, rows : rows + 1, :]
    code_down1 = side[1, rows + 1 : rows + 2, :]
    code_up2 = side[2, rows : rows + 1, :]
    flips = [code_down1, jnp.zeros_like(code_up1), code_up1, jnp.abs(code_up1 - code_up2)]
    row_y = lax.broadcasted_iota(jnp.int32, (seam, seam), 0)
    col_y = lax.broadcasted_iota(jnp.int32, (seam, seam), 1)
    eye = jnp.where(row_y == col_y, 1.0, 0.0)
    anti = jnp.where(row_y + col_y == seam - 1, 1.0, 0.0)
    perms = [(eye + (anti - eye) * flips[k]).astype(BF16) for k in range(4)]
    faces = []
    for k in range(4):
        block_k = side[k]
        if k != 1:
            hi = block_k.astype(BF16)
            rest = block_k - hi.astype(F32)
            mid = rest.astype(BF16)
            low = (rest - mid.astype(F32)).astype(BF16)
            block_k = dot(hi, perms[k]) + dot(mid, perms[k]) + dot(low, perms[k])
        for r in range(rows):
            faces.append(block_k[r : r + 1, :])

    lane = lax.broadcasted_iota(jnp.int32, (1, seam), 1).astype(F32)

    for k in (1, 2, 0, 3):
        if k == 1:
            arrived(emat.at[slot_other], e_recv.at[slot_other])
            for d in range(1, specs):
                src = lax.rem(s + d, specs)
                arrived(gath.at[slot_own, src], a_recv.at[slot_own, src])
            for src in range(specs):
                arrived(gath.at[slot_other, src], a_recv.at[slot_other, src])
        elif k != 2:
            arrived(emat.at[k], e_recv.at[k])
            for src in range(specs):
                arrived(gath.at[k, src], a_recv.at[k, src])
        field = [[gath[k, src, r] for src in range(specs)] for r in range(rows)]
        field = [jnp.concatenate(parts, axis=0) for parts in field]
        if k != 1:
            turned = dot(jnp.concatenate(field, axis=0), perms[k]).astype(BF16)
            field = [turned[r * species : (r + 1) * species] for r in range(rows)]
        chem = dot(emat[k], jnp.concatenate(field, axis=1))
        count = side[k, rows + 2 : rows + 3, :]
        place = lane + flips[k] * (seam - 1 - 2 * lane)
        for r in range(rows):
            active = (place + float(r * seam)) < count
            term = chem[:, r * seam : (r + 1) * seam]
            state[k * rows + r] = field[r].astype(F32) + jnp.where(active, term, 0.0)

    total = 4 * rows
    group = 16
    shape = (group, seam)

    def advect(who, within):
        at = pl.multiple_of(who * species_dev + within, group)
        a = [state[r, pl.ds(at, group), :] for r in range(total)]
        for step in range(1, NSUB + 1):
            new = list(a)
            for r in range(step, total - step):
                rising = jnp.maximum(faces[r], 0.0)
                falling = jnp.minimum(faces[r - 1], 0.0)
                new[r] = a[r] + rising * (a[r + 1] - a[r]) + falling * (a[r] - a[r - 1])
            a = new
        for r in range(rows):
            ret[0, who, r, within : within + group, :] = a[rows + r].astype(BF16)
        upper = jnp.concatenate([a[2 * rows + r] for r in range(rows)], axis=0).astype(BF16)
        upper = dot(upper, perms[2]).astype(BF16)
        for r in range(rows):
            ret[1, who, r, within : within + group, :] = upper[r * group : (r + 1) * group]

    for i in range(specs):
        who = lax.rem(s + 1 + i, specs)
        for within in range(0, species_dev, group):
            advect(who, within)
        for j in range(2):
            q = lax.rem(p + 1 + j, 2)
            if i < specs - 1 or j == 0:
                send(ret.at[q, who], out.at[own_level], r_send.at[2 * i + j], r_recv.at[own_level], (2 * z + q, who))
    own_copy = pltpu.make_async_copy(ret.at[p, s], out.at[own_level], own_sem)
    own_copy.start()
    for d in range(1, levels):
        lev = lax.rem(own_level + d, levels)
        arrived(out.at[lev], r_recv.at[lev])
    own_copy.wait()
    for copy in sends:
        copy.wait_send()


def unpack(packed_hbm, out_hbm, packed, out, in_sem, out_sem):
    levels, rows, species_dev, seam = packed.shape
    halves = 2
    part = species_dev // halves
    stride = levels * rows
    pitch = padded_pitch(stride)
    loads = []
    for lev in range(levels):
        copy = pltpu.make_async_copy(packed_hbm.at[lev], packed.at[lev], in_sem.at[lev])
        copy.start()
        loads.append(copy)
    stores = []
    for h in range(halves):
        for lev in range(levels):
            if h == 0:
                loads[lev].wait()
            for r in range(rows):
                start = h * part * pitch + lev * rows + r
                out[pl.ds(start, part, pitch), :] = packed[lev, r, h * part : (h + 1) * part, :].astype(F32)
        span = pl.ds(h * part, part)
        copy = pltpu.make_async_copy(
            out.reshape(species_dev, pitch, seam).at[span, pl.ds(0, stride)], out_hbm.at[span], out_sem.at[h]
        )
        copy.start()
        stores.append(copy)
    for copy in stores:
        copy.wait()


def shards(tiles, specs, adjoint, section_first, section_second, jacobian, pattern, counts, courant, seam_codes):
    species_dev, levels, rows, seam = adjoint.shape
    species = jacobian.shape[2]
    assert levels == 2 * specs and tiles % 2 == 0 and rows >= NSUB
    side_rows = (rows + 3 + 7) // 8 * 8
    dma = pltpu.SemaphoreType.DMA
    out = pl.pallas_call(
        functools.partial(kernel, tiles, specs, levels, rows, species_dev, pattern.shape[2]),
        out_shape=jax.ShapeDtypeStruct((levels, rows, species_dev, seam), BF16),
        in_specs=[pl.BlockSpec(memory_space=pl.ANY)] * 8,
        out_specs=pl.BlockSpec(memory_space=pl.ANY),
        scratch_shapes=[
            pltpu.VMEM((species_dev * padded_pitch(levels * rows), seam), F32),
            pltpu.VMEM((3, 2, species, species), BF16),
            pltpu.VMEM(courant.shape, F32),
            pltpu.SMEM((1,) + pattern.shape[2:] + (levels,), jnp.int32),
            pltpu.SMEM(counts.shape, jnp.int32),
            pltpu.SMEM(seam_codes.shape, jnp.int32),
            pltpu.VMEM((levels, rows, species_dev, seam), BF16),
            pltpu.VMEM((4, specs, rows, species_dev, seam), BF16),
            pltpu.VMEM((2, species, species), BF16),
            pltpu.VMEM((4, species, species), BF16),
            pltpu.VMEM((2, side_rows, seam), F32),
            pltpu.VMEM((4, side_rows, seam), F32),
            pltpu.VMEM((4 * rows, species, seam), F32),
            pltpu.VMEM((2, specs, rows, species_dev, seam), BF16),
            dma((9,)),
            dma(()),
            dma((2, levels)),
            dma((4, specs)),
            dma((3,)),
            dma((4,)),
            dma((3,)),
            dma((4,)),
            dma((levels,)),
            dma((levels,)),
        ],
        compiler_params=pltpu.CompilerParams(
            collective_id=0, has_side_effects=True, vmem_limit_bytes=60 * 1024 * 1024
        ),
    )(
        adjoint.reshape(species_dev, levels * rows, seam),
        section_first, section_second, jacobian, courant, jnp.transpose(pattern, (0, 2, 3, 1)), counts, seam_codes,
    )
    size = species_dev * levels * rows
    final = pl.pallas_call(
        unpack,
        out_shape=jax.ShapeDtypeStruct((species_dev, levels * rows, seam), F32),
        in_specs=[pl.BlockSpec(memory_space=pl.ANY)],
        out_specs=pl.BlockSpec(memory_space=pl.ANY),
        scratch_shapes=[
            pltpu.VMEM((levels, rows, species_dev, seam), BF16),
            pltpu.VMEM((species_dev * padded_pitch(levels * rows), seam), F32),
            dma((levels,)),
            dma((2,)),
        ],
        compiler_params=pltpu.CompilerParams(vmem_limit_bytes=60 * 1024 * 1024),
        cost_estimate=pl.CostEstimate(flops=0, bytes_accessed=6 * size * seam, transcendentals=0),
    )(out)
    return final.reshape(species_dev, levels, rows, seam)


def solution(mesh):
    in_specs = (
        P("spec", None, "tile", None),
        P("tile", None, None, None),
        P("tile", None, None, None),
        P("tile", None, None, None),
        P("tile", None, None, None),
        P("tile", None),
        P(None, "tile", None),
        P("tile", None),
    )
    out_specs = P("spec", None, "tile", None)
    body = functools.partial(shards, mesh.shape["tile"], mesh.shape["spec"])
    return jax.shard_map(body, mesh=mesh, in_specs=in_specs, out_specs=out_specs, check_vma=False)
```
